32 devices in a mesh: src: 16 (over z, y, core), blk: 2 (over x).
Axes of the slice: x: 2, y: 2, z: 4, core: 2. Of those that a mesh axis runs over, the one named last changes fastest.
Arguments:
- source_points: bfloat16 [65536, 256], P(('src', 'blk')), may hold values from -40 to 40
- source_slot: int32 [32, 2048], P(('src', 'blk')), may hold values from 0 to 2047, each once within a row
- source_logw: float32 [65536], P(('src', 'blk')), may hold values from -2 to 2
- target_points: bfloat16 [2048, 256], P(('blk', 'src')), may hold values from -40 to 40
- target_logw: float32 [2048], P(('blk', 'src')), may hold values from -2 to 2
- target_pot: bfloat16 [2048], P(('blk', 'src')), may hold values from -6 to 6
- pair_mask: int32 [128, 4], P(('src', 'blk')), may hold values from 0 to 1, as said below
Outputs:
- source_pot: float32 [65536], P(('src', 'blk'))
- target_next: float32 [2048], P(('blk', 'src'))
The draws below stay inside these ranges and needn't reach their ends.
Inputs may be any that keep to these rules, and one draw needn't show every extreme that they name: `pair_mask`: each source block p lists target block (p // 4) mod 4, so every source block and every target block has a listed pair. `source_slot`: each row is a permutation of 0 to 2047.
All inputs are finite; a program needn't handle non-finite values.
Results may differ from the reference program's by a relative error of at most 0.00035.
Values may be sent and summed in bfloat16 or wider, within the bound.
A program may use at most 64 MiB of HBM per device.

```python
import math
import jax
import jax.numpy as jnp
from jax import lax

DIM = 256
BLOCK = 512
SB_DEV = 4
PTS_DEV = 2048
NDEV = 32
NS = 65536
NSB = 128
NTB = 4
NT = 2048


def scaled_cloud(key, count, low_scale, high_scale):
    key_rows, key_scale = jax.random.split(key)
    cloud = jax.random.truncated_normal(key_rows, -5.0, 5.0, (count, DIM), jnp.float32)
    scale_log = jax.random.uniform(key_scale, (count, 1), jnp.float32, math.log(low_scale), math.log(high_scale))
    return cloud * jnp.exp(scale_log)


def draw_source_points(key, part):
    key = jax.random.fold_in(key, 3)
    cloud = scaled_cloud(key, NS, 0.3, 3.0)
    return cloud.astype(jnp.bfloat16)


def draw_target_points(key, part):
    key = jax.random.fold_in(key, 5)
    cloud = scaled_cloud(key, NT, 0.3, 3.0)
    return cloud.astype(jnp.bfloat16)


def draw_pair_mask(key, part):
    key = jax.random.fold_in(key, 7)
    key_level, key_pick = jax.random.split(key)
    level_id = jax.random.randint(key_level, (NDEV, 1), 0, 5)
    limit_per = jnp.repeat(40 * jnp.left_shift(1, level_id), SB_DEV, axis=0)
    ticket = jax.random.randint(key_pick, (NSB, NTB), 0, 1000)
    rows_id = jnp.arange(NSB, dtype=jnp.int32)[:, None]
    cols_id = jnp.arange(NTB, dtype=jnp.int32)[None, :]
    forced = cols_id == rows_id // SB_DEV % NTB
    return jnp.where((ticket < limit_per) | forced, 1, 0).astype(jnp.int32)


def levels(own_key, dims, cuts, least, largest):
    gain, own = 1.0, jax.random.fold_in(own_key, 6)
    for position, parts in cuts:
        heights = jnp.exp(jax.random.uniform(jax.random.fold_in(own, position), (parts,), jnp.float32, least / len(cuts), largest / len(cuts)))
        gain = gain * jnp.repeat(heights, dims[position] // parts).reshape([-1 if axis == position else 1 for axis in range(len(dims))])
    return gain


def gaussian(rng, shape, scale, most, shards=(), kind=jnp.bfloat16):
    entries = jax.random.normal(rng, shape, jnp.float32) * scale
    if len(shards) > 0:
        entries = levels(rng, shape, shards, -0.22, 0.18) * entries
    return jnp.clip(entries, min=-most, max=most).astype(kind)


def setup_inputs(seed: int = 0) -> dict:
    splits = jax.random.split(jax.random.key(seed), 8)
    source_points = draw_source_points(jax.random.fold_in(splits[7], 71), 0)
    source_slot = jax.vmap(lambda own: jax.random.permutation(own, PTS_DEV))(jax.random.split(splits[1], NDEV)).reshape((NDEV, PTS_DEV)).astype(jnp.int32)
    source_logw = jnp.clip(jax.random.uniform(splits[2], (NS,), jnp.float32, -2.0, 2.0) * levels(splits[2], (NS,), ((0, 32),), -0.4, 0.0), -2.0, 2.0)
    target_points = draw_target_points(jax.random.fold_in(splits[7], 71), 0)
    target_logw = jnp.clip(jax.random.uniform(splits[4], (NT,), jnp.float32, -2.0, 2.0) * levels(splits[4], (NT,), ((0, 32),), -0.4, 0.0), -2.0, 2.0)
    target_pot = gaussian(splits[5], (NT,), 1.0, 6.0, ((0, 32),))
    pair_mask = draw_pair_mask(jax.random.fold_in(splits[7], 71), 0)
    return dict(source_points=source_points, source_slot=source_slot, source_logw=source_logw, target_points=target_points, target_logw=target_logw, target_pot=target_pot, pair_mask=pair_mask)


entropic_eps = 0.25
floor_value = -1.0e30


def square_norms(points):
    widened = points.astype(jnp.float32)
    return jnp.sum(widened * widened, axis=1)


def tile_cost(src_tile, src_norm, tgt_tile, tgt_norm):
    inner_prod = jnp.dot(src_tile, tgt_tile.T, preferred_element_type=jnp.float32)
    return (src_norm[:, None] + tgt_norm[None, :] - 2.0 * inner_prod) / DIM


def row_update(prior, scores):
    peak_val, total_val = prior
    new_peak = jnp.maximum(peak_val, jnp.max(scores, axis=1))
    new_total = total_val * jnp.exp(peak_val - new_peak) + jnp.sum(jnp.exp(scores - new_peak[:, None]), axis=1)
    return new_peak, new_total


def col_update(prior, scores):
    peak_val, total_val = prior
    new_peak = jnp.maximum(peak_val, jnp.max(scores, axis=0))
    new_total = total_val * jnp.exp(peak_val - new_peak) + jnp.sum(jnp.exp(scores - new_peak[None, :]), axis=0)
    return new_peak, new_total


def reference(source_points, source_slot, source_logw, target_points, target_logw, target_pot, pair_mask):
    dev_count = source_slot.shape[0]
    per_device = source_slot.shape[1]
    offsets = (jnp.arange(dev_count, dtype=jnp.int32) * per_device)[:, None]
    slot_order = (source_slot + offsets).reshape(-1).astype(jnp.int32)
    block_rows = source_points[slot_order]
    block_logw = source_logw[slot_order]
    source_norm = square_norms(block_rows)
    target_norm = square_norms(target_points)
    tgt_pot = target_pot.astype(jnp.float32)
    src_blocks = block_rows.shape[0] // BLOCK
    tgt_blocks = target_points.shape[0] // BLOCK
    rows_split = block_rows.reshape(src_blocks, BLOCK, block_rows.shape[1])
    norms_split = source_norm.reshape(src_blocks, BLOCK)
    block_ids = jnp.arange(tgt_blocks, dtype=jnp.int32)

    def row_block(inputs):
        src_tile, src_norm, listed = inputs

        def one_target(carry_state, tgt_id):
            def live(kept):
                tgt_tile = lax.dynamic_slice_in_dim(target_points, tgt_id * BLOCK, BLOCK, 0)
                tgt_norm = lax.dynamic_slice_in_dim(target_norm, tgt_id * BLOCK, BLOCK, 0)
                tgt_vals = lax.dynamic_slice_in_dim(tgt_pot, tgt_id * BLOCK, BLOCK, 0)
                scores = (tgt_vals[None, :] - tile_cost(src_tile, src_norm, tgt_tile, tgt_norm)) / entropic_eps
                return row_update(kept, scores)
            return lax.cond(listed[tgt_id] > 0, live, lambda kept: kept, carry_state), None

        start_state = (jnp.full((BLOCK,), floor_value, jnp.float32), jnp.zeros((BLOCK,), jnp.float32))
        (peak_val, total_val), _ = lax.scan(one_target, start_state, block_ids)
        return peak_val + jnp.log(total_val)

    row_lse = lax.map(row_block, (rows_split, norms_split, pair_mask)).reshape(-1)
    f_blocked = entropic_eps * block_logw - entropic_eps * row_lse
    source_pot = jnp.zeros_like(f_blocked).at[slot_order].set(f_blocked)

    def col_block(carry_state, inputs):
        src_tile, src_norm, src_pot, listed = inputs

        def one_target(inner_state, tgt_id):
            def live(kept):
                peak_all, total_all = kept
                tgt_tile = lax.dynamic_slice_in_dim(target_points, tgt_id * BLOCK, BLOCK, 0)
                tgt_norm = lax.dynamic_slice_in_dim(target_norm, tgt_id * BLOCK, BLOCK, 0)
                scores = (src_pot[:, None] - tile_cost(src_tile, src_norm, tgt_tile, tgt_norm)) / entropic_eps
                new_peak, new_total = col_update((peak_all[tgt_id], total_all[tgt_id]), scores)
                return peak_all.at[tgt_id].set(new_peak), total_all.at[tgt_id].set(new_total)
            return lax.cond(listed[tgt_id] > 0, live, lambda kept: kept, inner_state), None

        carry_state, _ = lax.scan(one_target, carry_state, block_ids)
        return carry_state, None

    start_cols = (jnp.full((tgt_blocks, BLOCK), floor_value, jnp.float32), jnp.zeros((tgt_blocks, BLOCK), jnp.float32))
    (col_peak, col_total), _ = lax.scan(col_block, start_cols, (rows_split, norms_split, f_blocked.reshape(src_blocks, BLOCK), pair_mask))
    target_next = entropic_eps * target_logw - entropic_eps * (col_peak.reshape(-1) + jnp.log(col_total.reshape(-1)))
    return source_pot, target_next
```

```python
import math
import functools

import jax
import jax.numpy as jnp
from jax import lax
from jax.experimental import pallas as pl
from jax.experimental.pallas import tpu as pltpu
from jax.sharding import PartitionSpec as P

BLOCK = 512
LANES = 128
CHUNK = 256
EPS = 0.25
FLOOR = -1e30
LOG2E = math.log2(math.e)
LN2 = math.log(2.0)


def dot_t(a, b):
    return lax.dot_general(a, b, (((1,), (1,)), ((), ())), preferred_element_type=jnp.float32)


def norm_row(points):
    wide = points.astype(jnp.float32)
    square = wide * wide
    high = square.astype(jnp.bfloat16)
    low = (square - high.astype(jnp.float32)).astype(jnp.bfloat16)
    ones = jnp.ones((8, points.shape[1]), jnp.bfloat16)
    return (dot_t(ones, high) + dot_t(ones, low))[0:1]


def column_of(row):
    return jnp.broadcast_to(row, (LANES, LANES)).T


def prepare_mask(slot_ref, pm_ref, mask_ref, ntb):
    pts = slot_ref.shape[1]
    nrow = pts // LANES
    nsb = pts // BLOCK
    slot = slot_ref[...]
    hits, highs = [], []
    for p in range(nsb):
        part = slot[:, p * BLOCK : (p + 1) * BLOCK]
        low = jnp.broadcast_to(part & (LANES - 1), (LANES, BLOCK))
        lane = lax.broadcasted_iota(jnp.int32, (LANES, BLOCK), 0)
        hits.append(jnp.where(low == lane, 1.0, 0.0).astype(jnp.bfloat16))
        high = jnp.broadcast_to(part >> 7, (nrow, BLOCK))
        highs.append(high == lax.broadcasted_iota(jnp.int32, (nrow, BLOCK), 0))
    for q in range(ntb):
        listed = jnp.zeros((nrow, LANES), jnp.float32)
        for p in range(nsb):
            value = pm_ref[p, q].astype(jnp.float32)
            picked = jnp.where(highs[p], value, 0.0).astype(jnp.bfloat16)
            listed = listed + dot_t(picked, hits[p])
        bias = jnp.where(listed > 0.5, 0.0, FLOOR)
        for a in range(nrow):
            mask_ref[q * nrow + a] = bias[a : a + 1]


def wide_row(ref, index):
    return jnp.concatenate([ref[index], ref[index + 1]], axis=1)


def row_pass(x_ref, t_ref, u_ref, mask_ref, logw_ref, pot_ref, g_ref, ntb):
    scale = LOG2E / 32.0
    nrow = x_ref.shape[0] // LANES
    group = min(ntb, 4)

    def one_chunk(ch, _):
        src = x_ref[pl.ds(pl.multiple_of(ch * CHUNK, CHUNK), CHUNK), :]

        def one_group(grp, state):
            peak, total = state
            for k in range(group):
                q = grp * group + k
                rows = pl.ds(pl.multiple_of(q * BLOCK, BLOCK), BLOCK)
                u = u_ref[rows, :]
                s = dot_t(t_ref[rows, :], src) + jnp.concatenate([u, u], axis=1)
                m = jnp.max(s, axis=0, keepdims=True)
                part = jnp.sum(jnp.exp2((s - m) * scale), axis=0, keepdims=True)
                m = m * scale + wide_row(mask_ref, q * nrow + 2 * ch)
                new = jnp.maximum(peak, m)
                total = total * jnp.exp2(peak - new) + part * jnp.exp2(m - new)
                peak = new
            return peak, total

        start = (jnp.full((1, CHUNK), FLOOR, jnp.float32), jnp.zeros((1, CHUNK), jnp.float32))
        if ntb == group:
            peak, total = one_group(0, start)
        else:
            peak, total = lax.fori_loop(0, ntb // group, one_group, start)
        lse = peak + jnp.log2(total)
        logw = wide_row(logw_ref, 2 * ch)
        g = (logw * LOG2E - lse) * (1.0 / scale)
        pot = EPS * (logw - lse * LN2 + norm_row(src) * (1.0 / 64.0))
        for h in range(2):
            cut = slice(h * LANES, (h + 1) * LANES)
            pot_ref[2 * ch + h] = pot[:, cut]
            g_ref[2 * ch + h] = g[:, cut]
        return 0

    lax.fori_loop(0, nrow // 2, one_chunk, 0)


def col_pass(x_ref, t_ref, mask_ref, g_ref, gcol_ref, out_ref, ntb):
    scale = LOG2E / 32.0
    pts = x_ref.shape[0]
    nrow = pts // LANES

    def one_block(q, _):
        for a in range(nrow):
            gcol_ref[a * LANES : (a + 1) * LANES, :] = column_of(g_ref[a] + mask_ref[q * nrow + a])

        def one_chunk(half, _):
            ch = q * (BLOCK // CHUNK) + half
            tgt = t_ref[pl.ds(pl.multiple_of(ch * CHUNK, CHUNK), CHUNK), :]
            peaks, totals = [], []
            for p in range(pts // BLOCK):
                g = gcol_ref[p * BLOCK : (p + 1) * BLOCK, :]
                s = dot_t(x_ref[p * BLOCK : (p + 1) * BLOCK, :], tgt) + jnp.concatenate([g, g], axis=1)
                m = jnp.max(s, axis=0, keepdims=True)
                totals.append(jnp.sum(jnp.exp2((s - m) * scale), axis=0, keepdims=True))
                peaks.append(m * scale)
            peak = functools.reduce(jnp.maximum, peaks)
            total = sum(l * jnp.exp2(m - peak) for m, l in zip(peaks, totals))
            lse = peak + jnp.log2(total)
            out_ref[2 * ch] = lse[:, :LANES]
            out_ref[2 * ch + 1] = lse[:, LANES:]
            return 0

        lax.fori_loop(0, BLOCK // CHUNK, one_chunk, 0)
        return 0

    lax.fori_loop(0, ntb, one_block, 0)


def compute_kernel(ntb, x_ref, slot_ref, logw_ref, t_ref, u_ref, pm_ref, pot_ref, out_ref, mask_ref, g_ref, ucol_ref, gcol_ref):
    prepare_mask(slot_ref, pm_ref, mask_ref, ntb)
    for a in range(u_ref.shape[0]):
        ucol_ref[a * LANES : (a + 1) * LANES, :] = column_of(u_ref[a])
    row_pass(x_ref, t_ref, ucol_ref, mask_ref, logw_ref, pot_ref, g_ref, ntb)
    col_pass(x_ref, t_ref, mask_ref, g_ref, gcol_ref, out_ref, ntb)


def body(source_points, source_slot, source_logw, target_points, target_logw, target_pot, pair_mask):
    axes = ("blk", "src")
    ndev = lax.axis_size("blk") * lax.axis_size("src")
    pts, dim = source_points.shape
    shard = target_points.shape[0]
    nt = shard * ndev
    ntb = nt // BLOCK
    nrow = pts // LANES
    wide = target_points.astype(jnp.float32)
    tnorm = jnp.sum(wide * wide, axis=1)
    u = target_pot.astype(jnp.float32) * 128.0 - 0.5 * tnorm
    t_all = lax.all_gather(target_points, axes, axis=0, tiled=True)
    u_all = lax.all_gather(u, axes, axis=0, tiled=True)
    vmem = pl.BlockSpec(memory_space=pltpu.VMEM)
    pot, lse = pl.pallas_call(
        functools.partial(compute_kernel, ntb),
        out_shape=(
            jax.ShapeDtypeStruct((nrow, 1, LANES), jnp.float32),
            jax.ShapeDtypeStruct((nt // LANES, 1, LANES), jnp.float32),
        ),
        in_specs=[vmem] * 5 + [pl.BlockSpec(memory_space=pltpu.SMEM)],
        out_specs=(vmem, vmem),
        scratch_shapes=[
            pltpu.VMEM((ntb * nrow, 1, LANES), jnp.float32),
            pltpu.VMEM((nrow, 1, LANES), jnp.float32),
            pltpu.VMEM((nt, LANES), jnp.float32),
            pltpu.VMEM((pts, LANES), jnp.float32),
        ],
        compiler_params=pltpu.CompilerParams(vmem_limit_bytes=48 * 1024 * 1024),
    )(
        source_points,
        source_slot,
        source_logw.reshape(nrow, 1, LANES),
        t_all,
        u_all.reshape(nt // LANES, 1, LANES),
        pair_mask,
    )
    parts = lax.all_to_all(lse.reshape(ndev, shard), axes, 0, 0, tiled=True)
    peak = jnp.max(parts, axis=0)
    total = jnp.sum(jnp.exp2(parts - peak), axis=0)
    col = (peak + jnp.log2(total)) * LN2 - tnorm * (1.0 / 64.0)
    return pot.reshape(pts), EPS * target_logw - EPS * col


def solution(mesh):
    in_specs = (
        P(("src", "blk"), None),
        P(("src", "blk"), None),
        P(("src", "blk")),
        P(("blk", "src"), None),
        P(("blk", "src")),
        P(("blk", "src")),
        P(("src", "blk"), None),
    )
    out_specs = (P(("src", "blk")), P(("blk", "src")))
    return jax.shard_map(body, mesh=mesh, in_specs=in_specs, out_specs=out_specs, check_vma=False)
```

```python
import math
import functools

import jax
import jax.numpy as jnp
from jax import lax
from jax.experimental import pallas as pl
from jax.experimental.pallas import tpu as pltpu
from jax.sharding import PartitionSpec as P

BLOCK = 512
LANES = 128
CHUNK = 256
EPS = 0.25
FLOOR = -1e30
LOG2E = math.log2(math.e)
LN2 = math.log(2.0)


def dot_t(a, b):
    return lax.dot_general(a, b, (((1,), (1,)), ((), ())), preferred_element_type=jnp.float32)


def norm_row(points):
    wide = points.astype(jnp.float32)
    square = wide * wide
    high = square.astype(jnp.bfloat16)
    low = (square - high.astype(jnp.float32)).astype(jnp.bfloat16)
    ones = jnp.ones((8, points.shape[1]), jnp.bfloat16)
    return (dot_t(ones, high) + dot_t(ones, low))[0:1]


def column_of(row):
    return jnp.broadcast_to(row, (LANES, LANES)).T


def prepare_mask(slot_ref, pm_ref, mask_ref, ntb):
    pts = slot_ref.shape[1]
    nrow = pts // LANES
    nsb = pts // BLOCK
    slot = slot_ref[...]
    hits, highs = [], []
    for p in range(nsb):
        part = slot[:, p * BLOCK : (p + 1) * BLOCK]
        low = jnp.broadcast_to(part & (LANES - 1), (LANES, BLOCK))
        lane = lax.broadcasted_iota(jnp.int32, (LANES, BLOCK), 0)
        hits.append(jnp.where(low == lane, 1.0, 0.0).astype(jnp.bfloat16))
        high = jnp.broadcast_to(part >> 7, (nrow, BLOCK))
        highs.append(high == lax.broadcasted_iota(jnp.int32, (nrow, BLOCK), 0))
    for q in range(ntb):
        listed = jnp.zeros((nrow, LANES), jnp.float32)
        for p in range(nsb):
            value = pm_ref[p, q].astype(jnp.float32)
            picked = jnp.where(highs[p], value, 0.0).astype(jnp.bfloat16)
            listed = listed + dot_t(picked, hits[p])
        bias = jnp.where(listed > 0.5, 0.0, FLOOR)
        for a in range(nrow):
            mask_ref[q * nrow + a] = bias[a : a + 1]


def wide_row(ref, index):
    return jnp.concatenate([ref[index], ref[index + 1]], axis=1)


def row_pass(x_ref, t_ref, u_ref, mask_ref, logw_ref, pot_ref, g_ref, ntb):
    scale = LOG2E / 32.0
    nrow = x_ref.shape[0] // LANES
    group = min(ntb, 4)

    def one_chunk(ch, _):
        src = x_ref[pl.ds(pl.multiple_of(ch * CHUNK, CHUNK), CHUNK), :]

        def one_group(grp, state):
            peak, total = state
            for k in range(group):
                q = grp * group + k
                rows = pl.ds(pl.multiple_of(q * BLOCK, BLOCK), BLOCK)
                u = u_ref[rows, :]
                s = dot_t(t_ref[rows, :], src) + jnp.concatenate([u, u], axis=1)
                m = jnp.max(s, axis=0, keepdims=True)
                part = jnp.sum(jnp.exp2((s - m) * scale), axis=0, keepdims=True)
                m = m * scale + wide_row(mask_ref, q * nrow + 2 * ch)
                new = jnp.maximum(peak, m)
                total = total * jnp.exp2(peak - new) + part * jnp.exp2(m - new)
                peak = new
            return peak, total

        start = (jnp.full((1, CHUNK), FLOOR, jnp.float32), jnp.zeros((1, CHUNK), jnp.float32))
        if ntb == group:
            peak, total = one_group(0, start)
        else:
            peak, total = lax.fori_loop(0, ntb // group, one_group, start)
        lse = peak + jnp.log2(total)
        logw = wide_row(logw_ref, 2 * ch)
        g = (logw * LOG2E - lse) * (1.0 / scale)
        pot = EPS * (logw - lse * LN2 + norm_row(src) * (1.0 / 64.0))
        for h in range(2):
            cut = slice(h * LANES, (h + 1) * LANES)
            pot_ref[2 * ch + h] = pot[:, cut]
            g_ref[2 * ch + h] = g[:, cut]
        return 0

    lax.fori_loop(0, nrow // 2, one_chunk, 0)


def col_pass(x_ref, t_ref, mask_ref, g_ref, gcol_ref, out_ref, ntb):
    scale = LOG2E / 32.0
    pts = x_ref.shape[0]
    nrow = pts // LANES

    def one_block(q, _):
        for a in range(nrow):
            gcol_ref[a * LANES : (a + 1) * LANES, :] = column_of(g_ref[a] + mask_ref[q * nrow + a])

        def one_chunk(half, _):
            ch = q * (BLOCK // CHUNK) + half
            tgt = t_ref[pl.ds(pl.multiple_of(ch * CHUNK, CHUNK), CHUNK), :]
            peaks, totals = [], []
            for p in range(pts // BLOCK):
                g = gcol_ref[p * BLOCK : (p + 1) * BLOCK, :]
                s = dot_t(x_ref[p * BLOCK : (p + 1) * BLOCK, :], tgt) + jnp.concatenate([g, g], axis=1)
                m = jnp.max(s, axis=0, keepdims=True)
                totals.append(jnp.sum(jnp.exp2((s - m) * scale), axis=0, keepdims=True))
                peaks.append(m * scale)
            peak = functools.reduce(jnp.maximum, peaks)
            total = sum(l * jnp.exp2(m - peak) for m, l in zip(peaks, totals))
            lse = peak + jnp.log2(total)
            out_ref[2 * ch] = lse[:, :LANES]
            out_ref[2 * ch + 1] = lse[:, LANES:]
            return 0

        lax.fori_loop(0, BLOCK // CHUNK, one_chunk, 0)
        return 0

    lax.fori_loop(0, ntb, one_block, 0)


def fused_kernel(
    ntb, nsrc, nblk, x_hbm, slot_hbm, logw_hbm, tp_hbm, tpot_ref, tlogw_ref, pm_ref, pot_ref, next_ref,
    x_ref, slot_ref, logw_ref, t_ref, mask_ref, g_ref, ucol_ref, gcol_ref, u_ref, lse_ref, rec_ref,
    local_sem, pts_send, pts_recv, u_send, u_recv, lse_send, lse_recv,
):
    ndev = nsrc * nblk
    nz = nsrc // 4
    shard = tpot_ref.shape[1]
    per = LANES // shard
    s = lax.axis_index("src")
    b = lax.axis_index("blk")
    me = b * nsrc + s
    z, y, c = s // 4, s // 2 % 2, s % 2

    def rows_of(t):
        return t_ref.at[pl.ds(pl.multiple_of(t * shard, shard), shard), :]

    loads = [
        pltpu.make_async_copy(tp_hbm, rows_of(me), local_sem.at[0]),
        pltpu.make_async_copy(slot_hbm, slot_ref, local_sem.at[1]),
        pltpu.make_async_copy(logw_hbm, logw_ref, local_sem.at[2]),
        pltpu.make_async_copy(x_hbm, x_ref, local_sem.at[3]),
    ]
    for load in loads:
        load.start()

    barrier = pltpu.get_barrier_semaphore()

    def target(k):
        t = (me + k) % ndev
        return t, (t % nsrc, t // nsrc)

    def greet(k, _):
        pl.semaphore_signal(barrier, inc=1, device_id=target(k)[1], device_id_type=pl.DeviceIdType.MESH)
        return 0

    lax.fori_loop(1, ndev, greet, 0)

    loads[0].wait()
    tnorm = norm_row(rows_of(me)[...])
    u = tpot_ref[...].astype(jnp.float32) * 128.0 - 0.5 * tnorm
    if shard < LANES:
        u = jnp.concatenate([u, jnp.zeros((1, LANES - shard), jnp.float32)], axis=1)
    u_ref[me] = u
    loads[1].wait()
    prepare_mask(slot_ref, pm_ref, mask_ref, ntb)

    pl.semaphore_wait(barrier, ndev - 1)

    def send(t, dev_s, dev_b):
        pltpu.make_async_remote_copy(
            src_ref=rows_of(t), dst_ref=rows_of(t), send_sem=pts_send, recv_sem=pts_recv.at[t],
            device_id=(dev_s, dev_b), device_id_type=pl.DeviceIdType.MESH,
        ).start()

    def arrived(t):
        pltpu.make_async_copy(rows_of(t), rows_of(t), pts_recv.at[t]).wait()

    def slot_of(bb, zz, yy):
        return bb * nsrc + zz * 4 + yy * 2 + c

    def to_y(t):
        send(t, z * 4 + (1 - y) * 2 + c, b)

    def to_blk(t):
        for k in range(1, nblk):
            send(t, s, (b + k) % nblk)

    def to_core(t):
        send(t, z * 4 + y * 2 + (1 - c), b)

    for k in range(1, nz):
        send(me, (z + k) % nz * 4 + y * 2 + c, b)

    def send_u(k, _):
        pltpu.make_async_remote_copy(
            src_ref=u_ref.at[me], dst_ref=u_ref.at[me], send_sem=u_send, recv_sem=u_recv,
            device_id=target(k)[1], device_id_type=pl.DeviceIdType.MESH,
        ).start()
        return 0

    def plane(k, first):
        t = slot_of(b, (z + k) % nz, y)
        if not first:
            arrived(t)
        to_y(t)
        to_blk(t)
        to_core(t)
        return 0

    plane(0, True)
    lax.fori_loop(1, ndev, send_u, 0)
    lax.fori_loop(1, nz, lambda k, _: plane(k, False), 0)

    def pass_on(bb, zz, yy, onward):
        t = slot_of(bb, zz, yy)
        arrived(t)
        if onward is not None:
            onward(t)
        to_core(t)

    def drain(count):
        def one(_, carry):
            pltpu.make_async_copy(rows_of(me), rows_of(me), pts_send).wait()
            return carry

        lax.fori_loop(0, count, one, 0)

    @pl.when(c == 0)
    def _():
        def near(k, _):
            pass_on(b, (z + k) % nz, 1 - y, to_blk)
            return 0

        lax.fori_loop(0, nz, near, 0)

        def far(k, _):
            bb = (b + 1 + k // nz) % nblk
            pass_on(bb, (z + k) % nz, y, None)
            pass_on(bb, (z + k) % nz, 1 - y, None)
            return 0

        lax.fori_loop(0, nz * (nblk - 1), far, 0)

    @pl.when(c == 1)
    def _():
        def near(k, _):
            pass_on((b + 1 + k // nz) % nblk, (z + k) % nz, y, to_y)
            return 0

        lax.fori_loop(0, nz * (nblk - 1), near, 0)

        def far(k, _):
            pass_on((b + k // nz) % nblk, (z + k) % nz, 1 - y, None)
            return 0

        lax.fori_loop(0, nz * nblk, far, 0)

    others = u_ref.at[pl.ds(0, ndev - 1)]
    pltpu.make_async_copy(others, others, u_recv).wait()
    for t in range(ndev):
        ucol_ref[t * shard : (t + 1) * shard, :] = column_of(u_ref[t])[:shard]

    def other_core(k, _):
        pltpu.make_async_copy(rows_of(me), rows_of(me), pts_recv.at[2 * k + 1 - c]).wait()
        return 0

    lax.fori_loop(0, ndev // 2, other_core, 0)
    loads[2].wait()
    loads[3].wait()

    row_pass(x_ref, t_ref, ucol_ref, mask_ref, logw_ref, pot_ref, g_ref, ntb)
    col_pass(x_ref, t_ref, mask_ref, g_ref, gcol_ref, lse_ref, ntb)

    rec_ref[me] = lse_ref[me // per]

    def send_lse(k, _):
        t, where = target(k)
        pltpu.make_async_remote_copy(
            src_ref=lse_ref.at[t // per], dst_ref=rec_ref.at[me], send_sem=lse_send, recv_sem=lse_recv,
            device_id=where, device_id_type=pl.DeviceIdType.MESH,
        ).start()
        return 0

    lax.fori_loop(1, ndev, send_lse, 0)
    @pl.when(c == 0)
    def _():
        drain(nz - 1 + nz + 2 * nz * (nblk - 1) + 2 * nz * nblk)

    @pl.when(c == 1)
    def _():
        drain(nz - 1 + nz * (nblk - 1) + nz * nblk + 2 * nz * nblk)

    pltpu.make_async_copy(others, others, u_send).wait()
    received = rec_ref.at[pl.ds(0, ndev - 1)]
    pltpu.make_async_copy(received, received, lse_recv).wait()
    pltpu.make_async_copy(received, received, lse_send).wait()
    parts = rec_ref[...]
    peak = jnp.max(parts, axis=0)
    total = jnp.sum(jnp.exp2(parts - peak[None]), axis=0)
    lse = peak + jnp.log2(total)
    mine = lse[:, :shard]
    for k in range(1, per):
        mine = jnp.where(s % per == k, lse[:, k * shard : (k + 1) * shard], mine)
    next_ref[...] = EPS * (tlogw_ref[...] - mine * LN2 + tnorm * (1.0 / 64.0))


def body(source_points, source_slot, source_logw, target_points, target_logw, target_pot, pair_mask):
    nsrc, nblk = lax.axis_size("src"), lax.axis_size("blk")
    ndev = nsrc * nblk
    pts, dim = source_points.shape
    shard = target_points.shape[0]
    nt = shard * ndev
    ntb = nt // BLOCK
    nrow = pts // LANES
    vmem = pl.BlockSpec(memory_space=pltpu.VMEM)
    hbm = pl.BlockSpec(memory_space=pl.ANY)
    f32 = jnp.float32
    pot, fresh = pl.pallas_call(
        functools.partial(fused_kernel, ntb, nsrc, nblk),
        out_shape=(jax.ShapeDtypeStruct((nrow, 1, LANES), f32), jax.ShapeDtypeStruct((1, shard), f32)),
        in_specs=[hbm] * 4 + [vmem] * 2 + [pl.BlockSpec(memory_space=pltpu.SMEM)],
        out_specs=(vmem, vmem),
        scratch_shapes=[
            pltpu.VMEM((pts, dim), jnp.bfloat16),
            pltpu.VMEM((1, pts), jnp.int32),
            pltpu.VMEM((nrow, 1, LANES), f32),
            pltpu.VMEM((nt, dim), jnp.bfloat16),
            pltpu.VMEM((ntb * nrow, 1, LANES), f32),
            pltpu.VMEM((nrow, 1, LANES), f32),
            pltpu.VMEM((nt, LANES), f32),
            pltpu.VMEM((pts, LANES), f32),
            pltpu.VMEM((ndev, 1, LANES), f32),
            pltpu.VMEM((nt // LANES, 1, LANES), f32),
            pltpu.VMEM((ndev, 1, LANES), f32),
            pltpu.SemaphoreType.DMA((4,)),
            pltpu.SemaphoreType.DMA,
            pltpu.SemaphoreType.DMA((ndev,)),
            pltpu.SemaphoreType.DMA,
            pltpu.SemaphoreType.DMA,
            pltpu.SemaphoreType.DMA,
            pltpu.SemaphoreType.DMA,
        ],
        compiler_params=pltpu.CompilerParams(
            collective_id=0, has_side_effects=True, vmem_limit_bytes=48 * 1024 * 1024
        ),
    )(
        source_points,
        source_slot,
        source_logw.reshape(nrow, 1, LANES),
        target_points,
        target_pot.reshape(1, shard),
        target_logw.reshape(1, shard),
        pair_mask,
    )
    return pot.reshape(pts), fresh.reshape(shard)


def solution(mesh):
    in_specs = (
        P(("src", "blk"), None),
        P(("src", "blk"), None),
        P(("src", "blk")),
        P(("blk", "src"), None),
        P(("blk", "src")),
        P(("blk", "src")),
        P(("src", "blk"), None),
    )
    out_specs = (P(("src", "blk")), P(("blk", "src")))
    return jax.shard_map(body, mesh=mesh, in_specs=in_specs, out_specs=out_specs, check_vma=False)
```

```python
import math
import functools

import jax
import jax.numpy as jnp
from jax import lax
from jax.experimental import pallas as pl
from jax.experimental.pallas import tpu as pltpu
from jax.sharding import PartitionSpec as P

BLOCK = 512
LANES = 128
CHUNK = 256
EPS = 0.25
FLOOR = -1e30
LOG2E = math.log2(math.e)
LN2 = math.log(2.0)


def dot_t(a, b):
    return lax.dot_general(a, b, (((1,), (1,)), ((), ())), preferred_element_type=jnp.float32)


def norm_row(points):
    wide = points.astype(jnp.float32)
    square = wide * wide
    high = square.astype(jnp.bfloat16)
    low = (square - high.astype(jnp.float32)).astype(jnp.bfloat16)
    ones = jnp.ones((8, points.shape[1]), jnp.bfloat16)
    return (dot_t(ones, high) + dot_t(ones, low))[0:1]


def column_of(row):
    return jnp.broadcast_to(row, (LANES, LANES)).T


def prepare_mask(slot_ref, pm_ref, mask_ref, ntb):
    pts = slot_ref.shape[1]
    nrow = pts // LANES
    nsb = pts // BLOCK
    slot = slot_ref[...]
    hits, highs = [], []
    for p in range(nsb):
        part = slot[:, p * BLOCK : (p + 1) * BLOCK]
        low = jnp.broadcast_to(part & (LANES - 1), (LANES, BLOCK))
        lane = lax.broadcasted_iota(jnp.int32, (LANES, BLOCK), 0)
        hits.append(jnp.where(low == lane, 1.0, 0.0).astype(jnp.bfloat16))
        high = jnp.broadcast_to(part >> 7, (nrow, BLOCK))
        highs.append(high == lax.broadcasted_iota(jnp.int32, (nrow, BLOCK), 0))
    for q in range(ntb):
        listed = jnp.zeros((nrow, LANES), jnp.float32)
        for p in range(nsb):
            value = pm_ref[p, q].astype(jnp.float32)
            picked = jnp.where(highs[p], value, 0.0).astype(jnp.bfloat16)
            listed = listed + dot_t(picked, hits[p])
        bias = jnp.where(listed > 0.5, 0.0, FLOOR)
        for a in range(nrow):
            mask_ref[q * nrow + a] = bias[a : a + 1]


def wide_row(ref, index):
    return jnp.concatenate([ref[index], ref[index + 1]], axis=1)


def row_phase(x_ref, t_ref, u_ref, mask_ref, peak_ref, total_ref, base, count, ntb):
    scale = LOG2E / 32.0
    nrow = x_ref.shape[0] // LANES
    group = min(count, 4)

    def one_chunk(ch, _):
        src = x_ref[pl.ds(pl.multiple_of(ch * CHUNK, CHUNK), CHUNK), :]

        def one_group(grp, state):
            peak, total = state
            for k in range(group):
                piece = base + grp * group + k
                rows = pl.ds(pl.multiple_of(piece * CHUNK, CHUNK), CHUNK)
                u = u_ref[rows, :]
                s = dot_t(t_ref[rows, :], src) + jnp.concatenate([u, u], axis=1)
                m = jnp.max(s, axis=0, keepdims=True)
                part = jnp.sum(jnp.exp2((s - m) * scale), axis=0, keepdims=True)
                m = m * scale + wide_row(mask_ref, piece % ntb * nrow + 2 * ch)
                new = jnp.maximum(peak, m)
                total = total * jnp.exp2(peak - new) + part * jnp.exp2(m - new)
                peak = new
            return peak, total

        state = (wide_row(peak_ref, 2 * ch), wide_row(total_ref, 2 * ch))
        if count == group:
            peak, total = one_group(0, state)
        else:
            peak, total = lax.fori_loop(0, count // group, one_group, state)
        for h in range(2):
            cut = slice(h * LANES, (h + 1) * LANES)
            peak_ref[2 * ch + h] = peak[:, cut]
            total_ref[2 * ch + h] = total[:, cut]
        return 0

    lax.fori_loop(0, nrow // 2, one_chunk, 0)


def row_finish(norm_ref, logw_ref, peak_ref, total_ref, pot_ref, g_ref):
    scale = LOG2E / 32.0
    lse = peak_ref[...] + jnp.log2(total_ref[...])
    logw = logw_ref[...]
    g_ref[...] = (logw * LOG2E - lse) * (1.0 / scale)
    pot_ref[...] = EPS * (logw - lse * LN2 + norm_ref[...] * (1.0 / 64.0))


def col_pass(x_ref, t_ref, mask_ref, g_ref, gcol_ref, out_ref, ntb):
    scale = LOG2E / 32.0
    pts = x_ref.shape[0]
    nrow = pts // LANES

    def one_block(q, _):
        for a in range(nrow):
            gcol_ref[a * LANES : (a + 1) * LANES, :] = column_of(g_ref[a] + mask_ref[q * nrow + a])

        def one_chunk(half, _):
            ch = half * ntb + q
            tgt = t_ref[pl.ds(pl.multiple_of(ch * CHUNK, CHUNK), CHUNK), :]
            peaks, totals = [], []
            for p in range(pts // BLOCK):
                g = gcol_ref[p * BLOCK : (p + 1) * BLOCK, :]
                s = dot_t(x_ref[p * BLOCK : (p + 1) * BLOCK, :], tgt) + jnp.concatenate([g, g], axis=1)
                m = jnp.max(s, axis=0, keepdims=True)
                totals.append(jnp.sum(jnp.exp2((s - m) * scale), axis=0, keepdims=True))
                peaks.append(m * scale)
            peak = functools.reduce(jnp.maximum, peaks)
            total = sum(l * jnp.exp2(m - peak) for m, l in zip(peaks, totals))
            lse = peak + jnp.log2(total)
            out_ref[2 * ch] = lse[:, :LANES]
            out_ref[2 * ch + 1] = lse[:, LANES:]
            return 0

        lax.fori_loop(0, BLOCK // CHUNK, one_chunk, 0)
        return 0

    lax.fori_loop(0, ntb, one_block, 0)


def merged(parts):
    peak = jnp.max(parts, axis=0)
    return peak + jnp.log2(jnp.sum(jnp.exp2(parts - peak[None]), axis=0))


def fused_kernel(
    ntb, nsrc, nblk, x_hbm, slot_hbm, logw_hbm, tp_hbm, tpot_ref, tlogw_ref, pm_ref, pot_ref, next_ref,
    x_ref, slot_ref, logw_ref, t_ref, mask_ref, g_ref, ucol_ref, gcol_ref, u_ref, lse_ref, rec_ref,
    mid_ref, last_ref, norm_ref, peak_ref, total_ref,
    local_sem, pts_send, pts_recv, u_send, u_recv, lse_send, lse_recv,
):
    ndev = nsrc * nblk
    nz = nsrc // 4
    nplane = 4 * nblk
    shard = tpot_ref.shape[1]
    per = LANES // shard
    keep = 2 * nz // per
    per_group = ntb // nblk
    s = lax.axis_index("src")
    b = lax.axis_index("blk")
    z, y, c = s // 4, s // 2 % 2, s % 2

    def slot_at(cc, bb, zz, yy):
        return ((cc * nblk + bb) * nz + zz) * 2 + yy

    me = slot_at(c, b, z, y)
    plane_me = (c * nblk + b) * 2 + y

    def rows_of(t):
        return t_ref.at[pl.ds(pl.multiple_of(t * shard, shard), shard), :]

    loads = [
        pltpu.make_async_copy(tp_hbm, rows_of(me), local_sem.at[0]),
        pltpu.make_async_copy(slot_hbm, slot_ref, local_sem.at[1]),
        pltpu.make_async_copy(logw_hbm, logw_ref, local_sem.at[2]),
        pltpu.make_async_copy(x_hbm, x_ref, local_sem.at[3]),
    ]
    for load in loads:
        load.start()

    barrier = pltpu.get_barrier_semaphore()
    mesh_id = pl.DeviceIdType.MESH

    def plane_peer(k):
        p = (plane_me + k) % nplane
        return p, (z * 4 + p % 2 * 2 + p // (2 * nblk), p // 2 % nblk)

    def z_peer(k):
        zz = (z + k) % nz
        return zz, (zz * 4 + y * 2 + c, b)

    for k in range(1, nz):
        pl.semaphore_signal(barrier, inc=1, device_id=z_peer(k)[1], device_id_type=mesh_id)
    for k in range(1, nplane):
        pl.semaphore_signal(barrier, inc=1, device_id=plane_peer(k)[1], device_id_type=mesh_id)

    loads[0].wait()
    tnorm = norm_row(rows_of(me)[...])
    u = tpot_ref[...].astype(jnp.float32) * 128.0 - 0.5 * tnorm
    if shard < LANES:
        u = jnp.concatenate([u, jnp.zeros((1, LANES - shard), jnp.float32)], axis=1)
    u_ref[plane_me * nz + z] = u

    pl.semaphore_wait(barrier, nplane + nz - 2)

    def send(t, dev_s, dev_b):
        pltpu.make_async_remote_copy(
            src_ref=rows_of(t), dst_ref=rows_of(t), send_sem=pts_send, recv_sem=pts_recv.at[t],
            device_id=(dev_s, dev_b), device_id_type=mesh_id,
        ).start()

    def arrived(t):
        pltpu.make_async_copy(rows_of(t), rows_of(t), pts_recv.at[t]).wait()

    def to_y(t):
        send(t, z * 4 + (1 - y) * 2 + c, b)

    def to_blk(t):
        for k in range(1, nblk):
            send(t, s, (b + k) % nblk)

    def to_core(t):
        send(t, z * 4 + y * 2 + (1 - c), b)

    def small(src, dst, send_sem, recv_sem, where):
        pltpu.make_async_remote_copy(
            src_ref=src, dst_ref=dst, send_sem=send_sem, recv_sem=recv_sem, device_id=where, device_id_type=mesh_id
        ).start()

    def rows_done(ref, count, sem):
        part = ref.at[pl.ds(0, count)]
        pltpu.make_async_copy(part, part, sem).wait()

    for k in range(1, nz):
        send(me, *z_peer(k)[1])
    for k in range(1, nz):
        mine = u_ref.at[plane_me * nz + z]
        small(mine, mine, u_send, u_recv.at[0], z_peer(k)[1])
    to_y(me)
    to_blk(me)
    to_core(me)

    loads[1].wait()
    prepare_mask(slot_ref, pm_ref, mask_ref, ntb)

    def plane(k, _):
        t = slot_at(c, b, (z + k) % nz, y)
        arrived(t)
        to_y(t)
        to_blk(t)
        to_core(t)
        return 0

    lax.fori_loop(1, nz, plane, 0)

    rows_done(u_ref, nz - 1, u_recv.at[0])
    for k in range(1, nplane):
        group = u_ref.at[pl.ds(plane_me * nz, nz)]
        small(group, group, u_send, u_recv.at[1], plane_peer(k)[1])

    loads[3].wait()
    for a in range(x_ref.shape[0] // CHUNK):
        norm = norm_row(x_ref[a * CHUNK : (a + 1) * CHUNK, :])
        norm_ref[2 * a] = norm[:, :LANES]
        norm_ref[2 * a + 1] = norm[:, LANES:]
    peak_ref[...] = jnp.full(peak_ref.shape, FLOOR, jnp.float32)
    total_ref[...] = jnp.zeros(total_ref.shape, jnp.float32)

    def pass_on(bb, zz, yy, onward):
        t = slot_at(c, bb, zz, yy)
        arrived(t)
        if onward is not None:
            onward(t)
        to_core(t)

    @pl.when(c == 0)
    def _():
        def near(k, _):
            pass_on(b, (z + k) % nz, 1 - y, to_blk)
            return 0

        lax.fori_loop(0, nz, near, 0)

    @pl.when(c == 1)
    def _():
        def near(k, _):
            pass_on((b + 1 + k // nz) % nblk, (z + k) % nz, y, to_y)
            return 0

        lax.fori_loop(0, nz * (nblk - 1), near, 0)

        def home(k, _):
            pass_on(b, (z + k) % nz, 1 - y, None)
            return 0

        lax.fori_loop(0, nz, home, 0)

    rows_done(u_ref, (nplane - 1) * nz, u_recv.at[1])
    for cb in range(2 * nblk):
        for zz in range(nz):
            for yy in range(2):
                t = (cb * nz + zz) * 2 + yy
                ucol_ref[t * shard : (t + 1) * shard, :] = column_of(u_ref[(cb * 2 + yy) * nz + zz])[:shard]

    def phase(base, count):
        row_phase(x_ref, t_ref, ucol_ref, mask_ref, peak_ref, total_ref, base, count, ntb)

    phase(c * ntb + b * per_group, per_group)

    def far(k, _):
        bb = (b + 1 + k // nz) % nblk
        @pl.when(c == 0)
        def _():
            pass_on(bb, (z + k) % nz, y, None)
        pass_on(bb, (z + k) % nz, 1 - y, None)
        return 0

    lax.fori_loop(0, nz * (nblk - 1), far, 0)
    for k in range(1, nblk):
        phase(c * ntb + (b + k) % nblk * per_group, per_group)

    def other_core(k, _):
        arrived((1 - c) * (ndev // 2) + k)
        return 0

    lax.fori_loop(0, ndev // 2, other_core, 0)
    phase((1 - c) * ntb, ntb)
    loads[2].wait()
    row_finish(norm_ref, logw_ref, peak_ref, total_ref, pot_ref, g_ref)
    col_pass(x_ref, t_ref, mask_ref, g_ref, gcol_ref, lse_ref, ntb)

    def span(p):
        return pl.ds(p * keep, keep)

    for k in range(1, nplane):
        p, where = plane_peer(k)
        small(lse_ref.at[span(p // 2)], rec_ref.at[span(plane_me)], lse_send.at[0], lse_recv.at[0], where)
    rec_ref[span(plane_me)] = lse_ref[span(plane_me // 2)]
    rows_done(rec_ref, (nplane - 1) * keep, lse_recv.at[0])
    mid_ref[...] = merged(rec_ref[...].reshape(nplane, keep, 1, LANES))
    for k in range(1, nz):
        zz, where = z_peer(k)
        small(mid_ref.at[zz * 2 // per], last_ref.at[z], lse_send.at[1], lse_recv.at[1], where)
    last_ref[z] = mid_ref[z * 2 // per]

    def drain(count):
        def one(_, carry):
            pltpu.make_async_copy(rows_of(me), rows_of(me), pts_send).wait()
            return carry

        lax.fori_loop(0, count, one, 0)

    @pl.when(c == 0)
    def _():
        drain(nz - 1 + nz + 2 * nz * (nblk - 1) + 2 * nz * nblk)

    @pl.when(c == 1)
    def _():
        drain(nz - 1 + nz * (nblk - 1) + nz * nblk + 2 * nz * nblk)

    rows_done(u_ref, ndev - 1, u_send)
    rows_done(rec_ref, (nplane - 1) * keep, lse_send.at[0])
    rows_done(last_ref, nz - 1, lse_recv.at[1])
    rows_done(last_ref, nz - 1, lse_send.at[1])
    lse = merged(last_ref[...])
    mine = lse[:, :shard]
    for k in range(1, per):
        mine = jnp.where((z * 2 + y) % per == k, lse[:, k * shard : (k + 1) * shard], mine)
    next_ref[...] = EPS * (tlogw_ref[...] - mine * LN2 + tnorm * (1.0 / 64.0))


def body(source_points, source_slot, source_logw, target_points, target_logw, target_pot, pair_mask):
    nsrc, nblk = lax.axis_size("src"), lax.axis_size("blk")
    ndev = nsrc * nblk
    pts, dim = source_points.shape
    shard = target_points.shape[0]
    nt = shard * ndev
    ntb = nt // BLOCK
    nrow = pts // LANES
    keep = nsrc * shard // 2 // LANES
    vmem = pl.BlockSpec(memory_space=pltpu.VMEM)
    hbm = pl.BlockSpec(memory_space=pltpu.HBM)
    f32 = jnp.float32
    pot, fresh = pl.pallas_call(
        functools.partial(fused_kernel, ntb, nsrc, nblk),
        out_shape=(jax.ShapeDtypeStruct((nrow, 1, LANES), f32), jax.ShapeDtypeStruct((1, shard), f32)),
        in_specs=[hbm] * 4 + [vmem] * 2 + [pl.BlockSpec(memory_space=pltpu.SMEM)],
        out_specs=(vmem, vmem),
        scratch_shapes=[
            pltpu.VMEM((pts, dim), jnp.bfloat16),
            pltpu.VMEM((1, pts), jnp.int32),
            pltpu.VMEM((nrow, 1, LANES), f32),
            pltpu.VMEM((nt, dim), jnp.bfloat16),
            pltpu.VMEM((ntb * nrow, 1, LANES), f32),
            pltpu.VMEM((nrow, 1, LANES), f32),
            pltpu.VMEM((nt, LANES), f32),
            pltpu.VMEM((pts, LANES), f32),
            pltpu.VMEM((ndev, 1, LANES), f32),
            pltpu.VMEM((nt // LANES, 1, LANES), f32),
            pltpu.VMEM((4 * nblk * keep, 1, LANES), f32),
            pltpu.VMEM((keep, 1, LANES), f32),
            pltpu.VMEM((nsrc // 4, 1, LANES), f32),
            pltpu.VMEM((nrow, 1, LANES), f32),
            pltpu.VMEM((nrow, 1, LANES), f32),
            pltpu.VMEM((nrow, 1, LANES), f32),
            pltpu.SemaphoreType.DMA((4,)),
            pltpu.SemaphoreType.DMA,
            pltpu.SemaphoreType.DMA((ndev,)),
            pltpu.SemaphoreType.DMA,
            pltpu.SemaphoreType.DMA((2,)),
            pltpu.SemaphoreType.DMA((2,)),
            pltpu.SemaphoreType.DMA((2,)),
        ],
        compiler_params=pltpu.CompilerParams(
            collective_id=0, has_side_effects=True, vmem_limit_bytes=63 * 1024 * 1024
        ),
    )(
        source_points,
        source_slot,
        source_logw.reshape(nrow, 1, LANES),
        target_points,
        target_pot.reshape(1, shard),
        target_logw.reshape(1, shard),
        pair_mask,
    )
    return pot.reshape(pts), fresh.reshape(shard)


def solution(mesh):
    in_specs = (
        P(("src", "blk"), None),
        P(("src", "blk"), None),
        P(("src", "blk")),
        P(("blk", "src"), None),
        P(("blk", "src")),
        P(("blk", "src")),
        P(("src", "blk"), None),
    )
    out_specs = (P(("src", "blk")), P(("blk", "src")))
    return jax.shard_map(body, mesh=mesh, in_specs=in_specs, out_specs=out_specs, check_vma=False)
```

```python
import math
import functools

import jax
import jax.numpy as jnp
from jax import lax
from jax.experimental import pallas as pl
from jax.experimental.pallas import tpu as pltpu
from jax.sharding import PartitionSpec as P

BLOCK = 512
LANES = 128
CHUNK = 256
EPS = 0.25
FLOOR = -1e30
LOG2E = math.log2(math.e)
LN2 = math.log(2.0)


def dot_t(a, b):
    return lax.dot_general(a, b, (((1,), (1,)), ((), ())), preferred_element_type=jnp.float32)


def norm_row(points):
    wide = points.astype(jnp.float32)
    square = wide * wide
    high = square.astype(jnp.bfloat16)
    low = (square - high.astype(jnp.float32)).astype(jnp.bfloat16)
    ones = jnp.ones((8, points.shape[1]), jnp.bfloat16)
    return (dot_t(ones, high) + dot_t(ones, low))[0:1]


def column_of(row):
    return jnp.broadcast_to(row, (LANES, LANES)).T


def prepare_mask(slot_ref, pm_ref, mask_ref, ntb):
    pts = slot_ref.shape[1]
    nrow = pts // LANES
    nsb = pts // BLOCK
    slot = slot_ref[...]
    hits, highs = [], []
    for p in range(nsb):
        part = slot[:, p * BLOCK : (p + 1) * BLOCK]
        low = jnp.broadcast_to(part & (LANES - 1), (LANES, BLOCK))
        lane = lax.broadcasted_iota(jnp.int32, (LANES, BLOCK), 0)
        hits.append(jnp.where(low == lane, 1.0, 0.0).astype(jnp.bfloat16))
        high = jnp.broadcast_to(part >> 7, (nrow, BLOCK))
        highs.append(high == lax.broadcasted_iota(jnp.int32, (nrow, BLOCK), 0))
    for q in range(ntb):
        listed = jnp.zeros((nrow, LANES), jnp.float32)
        for p in range(nsb):
            value = pm_ref[p, q].astype(jnp.float32)
            picked = jnp.where(highs[p], value, 0.0).astype(jnp.bfloat16)
            listed = listed + dot_t(picked, hits[p])
        bias = jnp.where(listed > 0.5, 0.0, FLOOR)
        for a in range(nrow):
            mask_ref[q * nrow + a] = bias[a : a + 1]


def wide_row(ref, index):
    return jnp.concatenate([ref[index], ref[index + 1]], axis=1)


def row_phase(x_ref, t_ref, u_ref, mask_ref, peak_ref, total_ref, base, count, ntb):
    scale = LOG2E / 32.0
    nrow = x_ref.shape[0] // LANES
    group = min(count, 4)

    def one_chunk(ch, _):
        src = x_ref[pl.ds(pl.multiple_of(ch * CHUNK, CHUNK), CHUNK), :]

        def one_group(grp, state):
            peak, total = state
            for k in range(group):
                piece = base + grp * group + k
                rows = pl.ds(pl.multiple_of(piece * CHUNK, CHUNK), CHUNK)
                u = u_ref[rows, :]
                s = dot_t(t_ref[rows, :], src) + jnp.concatenate([u, u], axis=1)
                m = jnp.max(s, axis=0, keepdims=True)
                part = jnp.sum(jnp.exp2((s - m) * scale), axis=0, keepdims=True)
                m = m * scale + wide_row(mask_ref, piece % ntb * nrow + 2 * ch)
                new = jnp.maximum(peak, m)
                total = total * jnp.exp2(peak - new) + part * jnp.exp2(m - new)
                peak = new
            return peak, total

        state = (wide_row(peak_ref, 2 * ch), wide_row(total_ref, 2 * ch))
        if count == group:
            peak, total = one_group(0, state)
        else:
            peak, total = lax.fori_loop(0, count // group, one_group, state)
        for h in range(2):
            cut = slice(h * LANES, (h + 1) * LANES)
            peak_ref[2 * ch + h] = peak[:, cut]
            total_ref[2 * ch + h] = total[:, cut]
        return 0

    lax.fori_loop(0, nrow // 2, one_chunk, 0, unroll=2)


def row_finish(norm_ref, logw_ref, peak_ref, total_ref, pot_ref, g_ref):
    scale = LOG2E / 32.0
    lse = peak_ref[...] + jnp.log2(total_ref[...])
    logw = logw_ref[...]
    g_ref[...] = (logw * LOG2E - lse) * (1.0 / scale)
    pot_ref[...] = EPS * (logw - lse * LN2 + norm_ref[...] * (1.0 / 64.0))


def col_pass(x_ref, t_ref, mask_ref, g_ref, gcol_ref, out_ref, ntb):
    scale = LOG2E / 32.0
    pts = x_ref.shape[0]
    nrow = pts // LANES

    def one_block(q, _):
        for a in range(nrow):
            gcol_ref[a * LANES : (a + 1) * LANES, :] = column_of(g_ref[a] + mask_ref[q * nrow + a])

        def one_chunk(half, _):
            ch = half * ntb + q
            tgt = t_ref[pl.ds(pl.multiple_of(ch * CHUNK, CHUNK), CHUNK), :]
            peaks, totals = [], []
            for p in range(pts // BLOCK):
                g = gcol_ref[p * BLOCK : (p + 1) * BLOCK, :]
                s = dot_t(x_ref[p * BLOCK : (p + 1) * BLOCK, :], tgt) + jnp.concatenate([g, g], axis=1)
                m = jnp.max(s, axis=0, keepdims=True)
                totals.append(jnp.sum(jnp.exp2((s - m) * scale), axis=0, keepdims=True))
                peaks.append(m * scale)
            peak = functools.reduce(jnp.maximum, peaks)
            total = sum(l * jnp.exp2(m - peak) for m, l in zip(peaks, totals))
            lse = peak + jnp.log2(total)
            out_ref[2 * ch] = lse[:, :LANES]
            out_ref[2 * ch + 1] = lse[:, LANES:]
            return 0

        lax.fori_loop(0, BLOCK // CHUNK, one_chunk, 0, unroll=True)
        return 0

    lax.fori_loop(0, ntb, one_block, 0)


def merged(parts):
    peak = jnp.max(parts, axis=0)
    return peak + jnp.log2(jnp.sum(jnp.exp2(parts - peak[None]), axis=0))


def fused_kernel(
    ntb, nsrc, nblk, x_hbm, slot_hbm, logw_hbm, tp_hbm, tpot_ref, tlogw_ref, pm_ref, pot_ref, next_ref,
    x_ref, slot_ref, logw_ref, t_ref, mask_ref, g_ref, ucol_ref, gcol_ref, u_ref, lse_ref, rec_ref,
    mid_ref, last_ref, norm_ref, peak_ref, total_ref,
    local_sem, pts_send, pts_recv, u_send, u_recv, lse_send, lse_recv,
):
    ndev = nsrc * nblk
    nz = nsrc // 4
    nplane = 4 * nblk
    shard = tpot_ref.shape[1]
    per = LANES // shard
    keep = 2 * nz // per
    per_group = ntb // nblk
    s = lax.axis_index("src")
    b = lax.axis_index("blk")
    z, y, c = s // 4, s // 2 % 2, s % 2

    def slot_at(cc, bb, zz, yy):
        return ((cc * nblk + bb) * nz + zz) * 2 + yy

    me = slot_at(c, b, z, y)
    plane_me = (c * nblk + b) * 2 + y

    def rows_of(t):
        return t_ref.at[pl.ds(pl.multiple_of(t * shard, shard), shard), :]

    loads = [
        pltpu.make_async_copy(tp_hbm, rows_of(me), local_sem.at[0]),
        pltpu.make_async_copy(slot_hbm, slot_ref, local_sem.at[1]),
        pltpu.make_async_copy(logw_hbm, logw_ref, local_sem.at[2]),
        pltpu.make_async_copy(x_hbm, x_ref, local_sem.at[3]),
    ]
    for load in loads:
        load.start()

    barrier = pltpu.get_barrier_semaphore()
    mesh_id = pl.DeviceIdType.MESH

    def plane_peer(k):
        p = (plane_me + k) % nplane
        return p, (z * 4 + p % 2 * 2 + p // (2 * nblk), p // 2 % nblk)

    def z_peer(k):
        zz = (z + k) % nz
        return zz, (zz * 4 + y * 2 + c, b)

    for k in range(1, nz):
        pl.semaphore_signal(barrier, inc=1, device_id=z_peer(k)[1], device_id_type=mesh_id)
    for k in range(1, nplane):
        pl.semaphore_signal(barrier, inc=1, device_id=plane_peer(k)[1], device_id_type=mesh_id)

    loads[0].wait()
    tnorm = norm_row(rows_of(me)[...])
    u = tpot_ref[...].astype(jnp.float32) * 128.0 - 0.5 * tnorm
    if shard < LANES:
        u = jnp.concatenate([u, jnp.zeros((1, LANES - shard), jnp.float32)], axis=1)
    u_ref[plane_me * nz + z] = u

    pl.semaphore_wait(barrier, nplane + nz - 2)

    def send(t, dev_s, dev_b):
        pltpu.make_async_remote_copy(
            src_ref=rows_of(t), dst_ref=rows_of(t), send_sem=pts_send, recv_sem=pts_recv.at[t],
            device_id=(dev_s, dev_b), device_id_type=mesh_id,
        ).start()

    def arrived(t):
        pltpu.make_async_copy(rows_of(t), rows_of(t), pts_recv.at[t]).wait()

    def to_y(t):
        send(t, z * 4 + (1 - y) * 2 + c, b)

    def to_blk(t):
        for k in range(1, nblk):
            send(t, s, (b + k) % nblk)

    def to_core(t):
        send(t, z * 4 + y * 2 + (1 - c), b)

    def small(src, dst, send_sem, recv_sem, where):
        pltpu.make_async_remote_copy(
            src_ref=src, dst_ref=dst, send_sem=send_sem, recv_sem=recv_sem, device_id=where, device_id_type=mesh_id
        ).start()

    def rows_done(ref, count, sem):
        part = ref.at[pl.ds(0, count)]
        pltpu.make_async_copy(part, part, sem).wait()

    for k in range(1, nz):
        send(me, *z_peer(k)[1])
    for k in range(1, nz):
        mine = u_ref.at[plane_me * nz + z]
        small(mine, mine, u_send, u_recv.at[0], z_peer(k)[1])
    to_y(me)
    to_blk(me)
    to_core(me)

    loads[1].wait()
    prepare_mask(slot_ref, pm_ref, mask_ref, ntb)

    def plane(k, _):
        t = slot_at(c, b, (z + k) % nz, y)
        arrived(t)
        to_y(t)
        to_blk(t)
        to_core(t)
        return 0

    lax.fori_loop(1, nz, plane, 0)

    rows_done(u_ref, nz - 1, u_recv.at[0])
    for k in range(1, nplane):
        group = u_ref.at[pl.ds(plane_me * nz, nz)]
        small(group, group, u_send, u_recv.at[1], plane_peer(k)[1])

    loads[3].wait()
    for a in range(x_ref.shape[0] // CHUNK):
        norm = norm_row(x_ref[a * CHUNK : (a + 1) * CHUNK, :])
        norm_ref[2 * a] = norm[:, :LANES]
        norm_ref[2 * a + 1] = norm[:, LANES:]
    peak_ref[...] = jnp.full(peak_ref.shape, FLOOR, jnp.float32)
    total_ref[...] = jnp.zeros(total_ref.shape, jnp.float32)

    def pass_on(bb, zz, yy, onward):
        t = slot_at(c, bb, zz, yy)
        arrived(t)
        if onward is not None:
            onward(t)
        to_core(t)

    @pl.when(c == 0)
    def _():
        def near(k, _):
            pass_on(b, (z + k) % nz, 1 - y, to_blk)
            return 0

        lax.fori_loop(0, nz, near, 0)

    @pl.when(c == 1)
    def _():
        def near(k, _):
            pass_on((b + 1 + k // nz) % nblk, (z + k) % nz, y, to_y)
            return 0

        lax.fori_loop(0, nz * (nblk - 1), near, 0)

        def home(k, _):
            pass_on(b, (z + k) % nz, 1 - y, None)
            return 0

        lax.fori_loop(0, nz, home, 0)

    rows_done(u_ref, (nplane - 1) * nz, u_recv.at[1])
    for cb in range(2 * nblk):
        for zz in range(nz):
            for yy in range(2):
                t = (cb * nz + zz) * 2 + yy
                ucol_ref[t * shard : (t + 1) * shard, :] = column_of(u_ref[(cb * 2 + yy) * nz + zz])[:shard]

    def phase(base, count):
        row_phase(x_ref, t_ref, ucol_ref, mask_ref, peak_ref, total_ref, base, count, ntb)

    phase(c * ntb + b * per_group, per_group)

    def far(k, _):
        bb = (b + 1 + k // nz) % nblk
        @pl.when(c == 0)
        def _():
            pass_on(bb, (z + k) % nz, y, None)
        pass_on(bb, (z + k) % nz, 1 - y, None)
        return 0

    lax.fori_loop(0, nz * (nblk - 1), far, 0)
    for k in range(1, nblk):
        phase(c * ntb + (b + k) % nblk * per_group, per_group)

    def other_core(k, _):
        arrived((1 - c) * (ndev // 2) + k)
        return 0

    lax.fori_loop(0, ndev // 2, other_core, 0)
    phase((1 - c) * ntb, ntb)
    loads[2].wait()
    row_finish(norm_ref, logw_ref, peak_ref, total_ref, pot_ref, g_ref)
    col_pass(x_ref, t_ref, mask_ref, g_ref, gcol_ref, lse_ref, ntb)

    def span(p):
        return pl.ds(p * keep, keep)

    for k in range(1, nplane):
        p, where = plane_peer(k)
        small(lse_ref.at[span(p // 2)], rec_ref.at[span(plane_me)], lse_send.at[0], lse_recv.at[0], where)
    rec_ref[span(plane_me)] = lse_ref[span(plane_me // 2)]
    rows_done(rec_ref, (nplane - 1) * keep, lse_recv.at[0])
    mid_ref[...] = merged(rec_ref[...].reshape(nplane, keep, 1, LANES))
    for k in range(1, nz):
        zz, where = z_peer(k)
        small(mid_ref.at[zz * 2 // per], last_ref.at[z], lse_send.at[1], lse_recv.at[1], where)
    last_ref[z] = mid_ref[z * 2 // per]

    def drain(count):
        def one(_, carry):
            pltpu.make_async_copy(rows_of(me), rows_of(me), pts_send).wait()
            return carry

        lax.fori_loop(0, count, one, 0)

    @pl.when(c == 0)
    def _():
        drain(nz - 1 + nz + 2 * nz * (nblk - 1) + 2 * nz * nblk)

    @pl.when(c == 1)
    def _():
        drain(nz - 1 + nz * (nblk - 1) + nz * nblk + 2 * nz * nblk)

    rows_done(u_ref, ndev - 1, u_send)
    rows_done(rec_ref, (nplane - 1) * keep, lse_send.at[0])
    rows_done(last_ref, nz - 1, lse_recv.at[1])
    rows_done(last_ref, nz - 1, lse_send.at[1])
    lse = merged(last_ref[...])
    mine = lse[:, :shard]
    for k in range(1, per):
        mine = jnp.where((z * 2 + y) % per == k, lse[:, k * shard : (k + 1) * shard], mine)
    next_ref[...] = EPS * (tlogw_ref[...] - mine * LN2 + tnorm * (1.0 / 64.0))


def body(source_points, source_slot, source_logw, target_points, target_logw, target_pot, pair_mask):
    nsrc, nblk = lax.axis_size("src"), lax.axis_size("blk")
    ndev = nsrc * nblk
    pts, dim = source_points.shape
    shard = target_points.shape[0]
    nt = shard * ndev
    ntb = nt // BLOCK
    nrow = pts // LANES
    keep = nsrc * shard // 2 // LANES
    vmem = pl.BlockSpec(memory_space=pltpu.VMEM)
    hbm = pl.BlockSpec(memory_space=pltpu.HBM)
    f32 = jnp.float32
    pot, fresh = pl.pallas_call(
        functools.partial(fused_kernel, ntb, nsrc, nblk),
        out_shape=(jax.ShapeDtypeStruct((nrow, 1, LANES), f32), jax.ShapeDtypeStruct((1, shard), f32)),
        in_specs=[hbm] * 4 + [vmem] * 2 + [pl.BlockSpec(memory_space=pltpu.SMEM)],
        out_specs=(vmem, vmem),
        scratch_shapes=[
            pltpu.VMEM((pts, dim), jnp.bfloat16),
            pltpu.VMEM((1, pts), jnp.int32),
            pltpu.VMEM((nrow, 1, LANES), f32),
            pltpu.VMEM((nt, dim), jnp.bfloat16),
            pltpu.VMEM((ntb * nrow, 1, LANES), f32),
            pltpu.VMEM((nrow, 1, LANES), f32),
            pltpu.VMEM((nt, LANES), f32),
            pltpu.VMEM((pts, LANES), f32),
            pltpu.VMEM((ndev, 1, LANES), f32),
            pltpu.VMEM((nt // LANES, 1, LANES), f32),
            pltpu.VMEM((4 * nblk * keep, 1, LANES), f32),
            pltpu.VMEM((keep, 1, LANES), f32),
            pltpu.VMEM((nsrc // 4, 1, LANES), f32),
            pltpu.VMEM((nrow, 1, LANES), f32),
            pltpu.VMEM((nrow, 1, LANES), f32),
            pltpu.VMEM((nrow, 1, LANES), f32),
            pltpu.SemaphoreType.DMA((4,)),
            pltpu.SemaphoreType.DMA,
            pltpu.SemaphoreType.DMA((ndev,)),
            pltpu.SemaphoreType.DMA,
            pltpu.SemaphoreType.DMA((2,)),
            pltpu.SemaphoreType.DMA((2,)),
            pltpu.SemaphoreType.DMA((2,)),
        ],
        compiler_params=pltpu.CompilerParams(
            collective_id=0, has_side_effects=True, vmem_limit_bytes=63 * 1024 * 1024
        ),
    )(
        source_points,
        source_slot,
        source_logw.reshape(nrow, 1, LANES),
        target_points,
        target_pot.reshape(1, shard),
        target_logw.reshape(1, shard),
        pair_mask,
    )
    return pot.reshape(pts), fresh.reshape(shard)


def solution(mesh):
    in_specs = (
        P(("src", "blk"), None),
        P(("src", "blk"), None),
        P(("src", "blk")),
        P(("blk", "src"), None),
        P(("blk", "src")),
        P(("blk", "src")),
        P(("src", "blk"), None),
    )
    out_specs = (P(("src", "blk")), P(("blk", "src")))
    return jax.shard_map(body, mesh=mesh, in_specs=in_specs, out_specs=out_specs, check_vma=False)
```
